32 devices in a mesh: rows: 4 (over y, x), cols: 8 (over z, core).
Axes of the slice: x: 2, y: 2, z: 4, core: 2. Of those that a mesh axis runs over, the one named last changes fastest.
Arguments:
- interaction: bfloat16 [16384, 8192], P('rows', 'cols'), may hold values from -0.09375 to 0.09375
- commands: bfloat16 [1024, 8192], P('rows', 'cols'), may hold values from -6 to 6
- slopes_measured: bfloat16 [16384, 1024], P(('rows', 'cols')), may hold values from -6 to 6
- frame_lag: int32 [1], replicated, may hold values from 1 to 256
- frame_count: int32 [1], replicated, may hold values from 256 to 1024
Outputs:
- lag_covariance: float32 [16384, 16384], P('rows', 'cols')
The draws below stay inside these ranges and needn't reach their ends.
All inputs are finite; a program needn't handle non-finite values.
Results may differ from the reference program's by a relative error of at most 0.004.
Values may be sent and summed in bfloat16 or wider, within the bound.
No kernel may reach another device: no remote copies, remote signals or barrier semaphores. Data moves between devices by JAX's collectives and lax.ppermute only.
A program may use at most 128 MiB of HBM per device.

```python
import math
import jax
import jax.numpy as jnp
from jax import lax

SLOPES = 16384
ACTUATORS = 8192
FRAMES = 1024


def spiked(values, stream_key, source, target, blocks, factor):
    def block_of(dim):
        return (jnp.arange(values.shape[dim]) // (values.shape[dim] // blocks)).reshape((-1,) + (1,) * (values.ndim - 1 - dim))

    near = jax.random.permutation(stream_key, blocks)[block_of(target)]
    second = (block_of(target) + blocks // 2) % blocks
    return jnp.where((block_of(source) == near) | (block_of(source) == second), factor * values, values)


def block_levels(own_key, dims, split, least, top_value):
    loudness = 1.0
    for dim, blocks in split:
        heights = jax.random.uniform(jax.random.fold_in(jax.random.fold_in(own_key, 6), dim), (blocks,), jnp.float32, least / len(split), top_value / len(split))
        loudness = loudness * jnp.repeat(jnp.exp(heights), dims[dim] // blocks).reshape((-1,) + (1,) * (len(dims) - 1 - dim))
    return loudness


def bell_draw(own_key, dims, spread, most, cuts=(), kind=jnp.bfloat16):
    gain = block_levels(own_key, dims, cuts, -0.22, 0.18) if cuts else 1.0
    result = jax.random.normal(own_key, dims, jnp.float32) * spread * gain
    return jnp.minimum(jnp.maximum(result, -most), most).astype(kind)


def gaussian_with(key, dims, width, bound, split, heavy, kind=jnp.bfloat16):
    values = width * jax.random.normal(key, dims, jnp.float32)
    if split:
        values = values * block_levels(key, dims, split, -0.22, 0.18)
    return jnp.clip(spiked(values, jax.random.fold_in(key, 3), *heavy), -bound, bound).astype(kind)


def setup_inputs(seed: int = 0) -> dict:
    splits = jax.random.split(jax.random.key(seed), 6)
    return {
        "interaction": gaussian_with(splits[0], (SLOPES, ACTUATORS), ACTUATORS ** -0.5, 0.09375, ((0, 4), (1, 8)), (1, 0, 8, 2.0)),
        "commands": bell_draw(splits[1], (FRAMES, ACTUATORS), 1.0, 6.0, ((0, 4), (1, 8))),
        "slopes_measured": bell_draw(splits[2], (SLOPES, FRAMES), 1.0, 6.0, ((0, 32),)),
        "frame_lag": jax.random.randint(splits[3], (1,), 1, FRAMES // 4 + 1).astype(jnp.int32),
        "frame_count": jax.random.randint(splits[4], (1,), FRAMES // 4, FRAMES + 1).astype(jnp.int32),
    }


def reference(interaction, commands, slopes_measured, frame_lag, frame_count):
    margin = FRAMES // 4
    padded = jnp.concatenate([jnp.zeros((margin, ACTUATORS), commands.dtype), commands], axis=0)
    delayed = lax.dynamic_slice_in_dim(padded, (margin - frame_lag[0]).astype(jnp.int32), FRAMES, 0)
    response = jnp.dot(interaction, delayed.T, preferred_element_type=jnp.float32)
    summed = response + slopes_measured.astype(jnp.float32)
    frame_index = jnp.arange(FRAMES, dtype=jnp.int32)
    openloop = jnp.where(frame_index[None, :] < frame_count[0], summed, 0.0).astype(jnp.bfloat16)
    advanced = jnp.concatenate([openloop[:, 1:], jnp.zeros((SLOPES, 1), jnp.bfloat16)], axis=1)
    scaling = 1.0 / math.sqrt(FRAMES)
    return jnp.dot(advanced, openloop.T, preferred_element_type=jnp.float32) * scaling
```

```python
import math
from functools import partial

import jax
import jax.numpy as jnp
import numpy as np
from jax import lax
from jax.experimental import pallas as pl
from jax.experimental.pallas import tpu as pltpu
from jax.sharding import Mesh, PartitionSpec as P

AXES = ("rows", "line", "core")
NT = (((1,), (1,)), ((), ()))


def tile_kernel(plan, scaling, base_ref, *refs):
    row_plan, col_plan, jobs = plan
    n_rows, n_cols = len(row_plan), len(col_plan)
    row_refs = refs[: 2 * n_rows]
    col_refs = refs[2 * n_rows : 2 * n_rows + n_cols]
    out_ref = refs[2 * n_rows + n_cols + 1]
    held, turned, tiles, row_sems, sems = refs[2 * n_rows + n_cols + 2 :]
    chunk = tiles.shape[1] // 2
    order = [a for i, (a, _) in enumerate(jobs) if i == 0 or jobs[i - 1][0] != a]

    def loads(turn):
        slot = turn % 2
        return [
            pltpu.make_async_copy(
                row_refs[2 * order[turn] + i], held.at[slot, pl.ds(i * chunk, chunk)], row_sems.at[slot, i]
            )
            for i in range(2)
        ]

    def stores(index):
        a, b = jobs[index]
        slot = index % 2
        half, row_at = row_plan[a]
        kind, col_at = col_plan[b]
        col = pl.multiple_of(base_ref[4 + kind] + col_at, 128)
        out = []
        for i in range(2):
            row = pl.multiple_of(base_ref[2 * half + i] + row_at, 8)
            out.append(
                pltpu.make_async_copy(
                    tiles.at[slot, pl.ds(i * chunk, chunk)],
                    out_ref.at[pl.ds(row, chunk), pl.ds(col, tiles.shape[2])],
                    sems.at[slot, i],
                )
            )
        return out

    for copy in loads(0):
        copy.start()
    for b in range(n_cols):
        block = col_refs[b][...].astype(jnp.float32)
        frame = lax.broadcasted_iota(jnp.int32, block.shape, 1)
        rolled = jnp.where(frame == 0, 0.0, pltpu.roll(block, 1, 1))
        turned[b] = rolled.T.astype(jnp.bfloat16)
    turn = -1
    for index, (a, b) in enumerate(jobs):
        if index == 0 or jobs[index - 1][0] != a:
            turn += 1
            for copy in loads(turn):
                copy.wait()
            if turn + 1 < len(order):
                for copy in loads(turn + 1):
                    copy.start()
        if index >= 2:
            for copy in stores(index - 2):
                copy.wait()
        tiles[index % 2] = scaling * jnp.dot(
            held[turn % 2], turned[b], preferred_element_type=jnp.float32
        )
        for copy in stores(index):
            copy.start()
    for index in range(max(0, len(jobs) - 2), len(jobs)):
        for copy in stores(index):
            copy.wait()


def covariance_part(covariance, base, pairs, scaling):
    rows, cols, jobs = [], [], []
    for row, col in pairs:
        for group, one in ((rows, row), (cols, col)):
            if not any(one is seen for seen in group):
                group.append(one)
        a = next(i for i, seen in enumerate(rows) if seen is row)
        jobs.append((a, next(i for i, seen in enumerate(cols) if seen is col)))
    jobs.sort()
    height, depth = rows[0][0][0].shape
    width = cols[0][0].shape[0]
    vmem, anywhere = pl.BlockSpec(memory_space=pltpu.VMEM), pl.BlockSpec(memory_space=pl.ANY)
    operands = [base, *(part for r in rows for part in r[0]), *(c[0] for c in cols), covariance]
    plan = ([r[1:] for r in rows], [c[1:] for c in cols], jobs)
    tiles = len(jobs) * 2 * height * width
    return pl.pallas_call(
        lambda *refs: tile_kernel(plan, scaling, *refs),
        out_shape=jax.ShapeDtypeStruct(covariance.shape, covariance.dtype),
        in_specs=[pl.BlockSpec(memory_space=pltpu.SMEM)]
        + [anywhere] * (2 * len(rows))
        + [vmem] * len(cols)
        + [anywhere],
        out_specs=anywhere,
        scratch_shapes=[
            pltpu.VMEM((2, 2 * height, depth), jnp.bfloat16),
            pltpu.VMEM((len(cols), depth, width), jnp.bfloat16),
            pltpu.VMEM((2, 2 * height, width), jnp.float32),
            pltpu.SemaphoreType.DMA((2, 2)),
            pltpu.SemaphoreType.DMA((2, 2)),
        ],
        input_output_aliases={len(operands) - 1: 0},
        compiler_params=pltpu.CompilerParams(vmem_limit_bytes=40 * 2**20),
        cost_estimate=pl.CostEstimate(flops=2 * tiles * depth, bytes_accessed=4 * tiles, transcendentals=0),
    )(*operands)


def empty_kernel(out_ref):
    pass


def tie(*values):
    return lax.optimization_barrier(values)


def local(frames, chunks, sizes, interaction, commands, slopes, frame_lag, frame_count):
    n_rows, n_line = sizes
    row = lax.axis_index("rows")
    place = lax.axis_index("line")
    core = lax.axis_index("core")
    all_frames = slopes.shape[1]
    block_rows, block_acts = interaction.shape
    half = block_rows // 2
    quarter = half // 2
    middle = n_line // 2 - 1
    side = (place > middle).astype(jnp.int32)
    inner = (place == middle) | (place == middle + 1)

    def flat(r, z, k):
        return (r * n_line + z) * 2 + k

    def move(value, hops):
        pairs = [(flat(*a), flat(*b)) for a, b in hops]
        return lax.ppermute(value, AXES, pairs)

    everyone = [(r, z, k) for r in range(n_rows) for z in range(n_line) for k in range(2)]

    def swap_core(value):
        return move(value, [((r, z, k), (r, z, 1 - k)) for r, z, k in everyone])

    block_frames = commands.shape[0]
    sources = [r for r in range(n_rows) if r * block_frames < frames]

    def cross(value, mask, wanted):
        return move(value, [((r, z, k), (r ^ mask, z, k)) for r, z, k in everyone if r in wanted])

    n_bits = n_rows.bit_length() - 1
    begun = []
    for bit in range(n_bits):
        begun.append(cross(commands, 1 << bit, sources))
    slab = slopes.shape[0]
    per_quarter = quarter // slab
    for i in range(per_quarter):
        hops = []
        for r in range(n_rows):
            for k in range(2):
                for o in range(2):
                    index = (k * 2 + o) * per_quarter + i
                    hops.append(((r, index // 2, index % 2), (r, middle + o, k)))
        begun.append(move(slopes[:, :frames], hops))
    begun.append(swap_core(interaction))
    begun = lax.optimization_barrier(begun)
    other = begun[-1]
    measured = begun[n_bits:-1]
    blocks = {0: commands}
    blocks.update({1 << bit: begun[bit] for bit in range(n_bits)})
    for mask in range(n_rows):
        ways = [1 << bit for bit in range(n_bits) if mask >> bit & 1]
        if len(ways) < 2:
            continue
        share = block_frames // len(ways)
        shares = [
            cross(blocks[mask ^ way][i * share : (i + 1) * share], way, [r ^ mask ^ way for r in sources])
            for i, way in enumerate(ways)
        ]
        blocks[mask] = jnp.concatenate(shares, 0)
    margin = all_frames // 4
    held = jnp.zeros((margin + n_rows * block_frames, block_acts), commands.dtype)
    for mask, block in blocks.items():
        held = lax.dynamic_update_slice_in_dim(held, block, margin + (row ^ mask) * block_frames, 0)
    delayed = lax.dynamic_slice_in_dim(held, margin - frame_lag[0], frames, 0)
    delayed_other = swap_core(delayed)

    chunk = quarter // chunks

    def response(offset):
        parts = [
            lax.dot_general(
                lax.dynamic_slice_in_dim(matrix, offset + at, chunk, 0),
                command,
                NT,
                preferred_element_type=jnp.float32,
            )
            for matrix, at, command in ((interaction, core * half, delayed), (other, core * half, delayed_other))
        ]
        return parts[0] + parts[1]

    def measured_part(j):
        first, stop = j * chunk, (j + 1) * chunk
        parts = [
            measured[i][max(first - i * slab, 0) : min(stop - i * slab, slab)]
            for i in range(per_quarter)
            if i * slab < stop and first < (i + 1) * slab
        ]
        return parts[0] if len(parts) == 1 else jnp.concatenate(parts, 0)

    last = n_line - 1
    inward = [
        [((r, z, k), (r, z + d, k)) for r in range(n_rows) for k in range(2) for z, d in ((i, 1), (last - i, -1))]
        for i in range(middle)
    ]
    outward = [[(b, a) for a, b in hops] for hops in reversed(inward)]
    across = [
        ((r, middle + o, k), (r, middle + 1 - o, k)) for r in range(n_rows) for k in range(2) for o in range(2)
    ]

    def exchange(value, finished):
        zeros = jnp.zeros((chunk, frames), jnp.bfloat16)
        if middle == 1:
            narrow = zeros if value is None else value.astype(jnp.bfloat16)
            moved = move(jnp.where(inner, zeros if finished is None else finished, narrow), inward[0] + outward[0])
            return moved, moved
        added = value
        if value is not None:
            for hops in inward:
                arrived = move(added.astype(jnp.bfloat16), hops)
                added = value + arrived.astype(jnp.float32)
        if finished is not None:
            for step, hops in enumerate(outward):
                reached = jnp.where(side == 1, place - middle - 1, middle - place)
                finished = jnp.where(reached == step + 1, move(finished, hops), finished)
        return (None if value is None else arrived), finished

    per_row = 2 * n_line // n_rows
    source = (2 * place + core) // per_row

    def spread(value, bit):
        step = 1 << bit
        hops = []
        for z in range(n_line):
            for k in range(2):
                s = (2 * z + k) // per_row
                hops += [((s ^ m, z, k), (s ^ m ^ step, z, k)) for m in range(step)]
        return jnp.where((row ^ source) // step == 1, move(value, hops), value)

    frame_index = lax.broadcasted_iota(jnp.int32, (chunk, frames), 1)
    valid = frame_index < frame_count[0]
    scaling = 1.0 / math.sqrt(all_frames)
    n_columns = n_rows * block_rows // (2 * n_line)
    pieces = half // n_columns
    covariance = pl.pallas_call(
        empty_kernel,
        out_shape=jax.ShapeDtypeStruct((block_rows, n_columns), jnp.float32),
        out_specs=pl.BlockSpec(memory_space=pl.ANY),
    )()
    near_at, far_at = side * quarter, (1 - side) * quarter
    own_at, other_at = core * half, (1 - core) * half
    column_at = (near_at, far_at) if pieces == 1 else (0, 0)
    base = jnp.stack(
        [own_at + near_at, own_at + far_at, other_at + near_at, other_at + far_at, *column_at]
    ).astype(jnp.int32)

    live = {
        "far": response(far_at),
        "covariance": covariance,
    }
    row_info, col_info, waiting = {}, {}, []
    n_steps = 2 * chunks + 2 + n_bits + (0 if pieces == 1 else 1)
    for h in range(n_steps + 1):
        live = dict(zip(live, lax.optimization_barrier(list(live.values()))))
        j, odd = h // 2, h % 2
        new = dict(live)
        into = live.pop("near" if odd else "far", None)
        new.pop("near" if odd else "far", None)
        finished = None
        if odd and j < chunks:
            total = live["far_value"] + live["arrived"].astype(jnp.float32)
            new.pop("far_value")
            new["crossed"] = move(total.astype(jnp.bfloat16), across)
        if odd and 1 <= j <= chunks:
            finished = new.pop("other_done")
        if not odd and 1 <= j <= chunks:
            part = measured_part(j - 1).astype(jnp.float32)
            total = live["near_value"] + live["arrived"].astype(jnp.float32)
            total = total + live["crossed"].astype(jnp.float32) + part
            for name in ("near_value", "crossed"):
                new.pop(name)
            finished = jnp.where(valid, total, 0.0).astype(jnp.bfloat16)
            new["other_done"] = move(finished, across)
        new.pop("arrived", None)
        if into is not None or finished is not None:
            arrived, done = exchange(into, finished)
            if into is not None:
                new["arrived"] = arrived
                new["near_value" if odd else "far_value"] = into
            if finished is not None:
                mine = finished if middle == 1 else None
                done = done if mine is None else jnp.where(inner, mine, done)
                new[("far_rows" if odd else "near_rows", j - 1)] = done
        for name, key, i in (("near_rows", 0, (h - 3) // 2), ("far_rows", 1, (h - 4) // 2)):
            if h >= 3 and (h % 2 == 1) == (key == 0) and 0 <= i < chunks:
                new["row", 0, i, key] = live[name, i]
                new["row", 1, i, key] = swap_core(live[name, i])
        if pieces == 1:
            begun = [(("near_rows", (h - 3) // 2), h >= 3 and odd), (("far_rows", (h - 4) // 2), h >= 4 and not odd)]
            for (name, i), now in begun:
                if now and i < chunks:
                    waiting.append([live[name, i], 0, int(name == "far_rows"), i])
        else:
            i = (h - 5) // 2
            if h >= 5 and odd and i < chunks:
                wanted = (2 * place + core) % per_row
                parts = [
                    jnp.where(wanted // pieces == core, live["row", 0, i, part], live["row", 1, i, part])
                    for part in range(2)
                ]
                waiting.append([jnp.where(wanted % pieces == side, *parts), 0, 0, i])
        for name in [key for key in live if key[0] == "moving"]:
            waiting.append([live[name], *name[1:]])
            new.pop(name)
        for value, bit, kind, i in waiting:
            value = spread(value, bit)
            new[("col", kind, i) if bit + 1 == n_bits else ("moving", bit + 1, kind, i)] = value
        waiting = []
        if j < chunks and not odd:
            new["near"] = response(near_at + j * chunk)
        if odd and j + 1 < chunks:
            new["far"] = response(far_at + (j + 1) * chunk)
        row_keys = [key[:3] for key in live if key[0] == "row" and key[3] == 1]
        col_keys = [key for key in live if key[0] == "col"]
        row_of = {key: ((live[*key, 0], live[*key, 1]), key[1], key[2] * chunk) for key in row_keys}
        col_of = {key: (live[key], key[1], key[2] * chunk) for key in col_keys}
        todo = [
            (row_of[a], col_of[b]) for b in col_keys for a in row_keys if (a, b) not in row_info
        ]
        row_info.update({(a, b): True for b in col_keys for a in row_keys})
        if todo:
            new["covariance"] = covariance_part(live["covariance"], base, todo, scaling)
        live = new
    return live["covariance"]


def solution(mesh, force=None, chunks=2):
    n_rows, n_cols = mesh.devices.shape
    line = Mesh(mesh.devices.reshape(n_rows, n_cols // 2, 2), AXES)
    sizes = (n_rows, n_cols // 2)

    def body(interaction, commands, slopes, frame_lag, frame_count):
        args = (interaction, commands, slopes, frame_lag, frame_count)
        unit = slopes.shape[1] // 8
        if force is not None:
            return local(force, chunks, sizes, *args)
        extents = [unit * i for i in range(3, 9)]
        which = jnp.clip((frame_count[0] + unit - 1) // unit - 3, 0, len(extents) - 1)
        return lax.switch(which, [partial(local, frames, chunks, sizes) for frames in extents], *args)

    both = ("line", "core")
    return jax.shard_map(
        body,
        mesh=line,
        in_specs=(P("rows", both), P("rows", both), P(AXES, None), P(), P()),
        out_specs=P("rows", both),
        check_vma=False,
    )
```

```python
import math
from functools import partial

import jax
import jax.numpy as jnp
import numpy as np
from jax import lax
from jax.experimental import pallas as pl
from jax.experimental.pallas import tpu as pltpu
from jax.sharding import Mesh, PartitionSpec as P

AXES = ("rows", "line", "core")
FREE = ("row", "col", "moving", "near_rows", "far_rows")
NT = (((1,), (1,)), ((), ()))


def tile_kernel(plan, scaling, base_ref, *refs):
    row_plan, col_plan, jobs = plan
    n_rows, n_cols = len(row_plan), len(col_plan)
    row_refs = refs[: 2 * n_rows]
    col_refs = refs[2 * n_rows : 2 * n_rows + n_cols]
    out_ref = refs[2 * n_rows + n_cols + 1]
    held, turned, tiles, row_sems, sems = refs[2 * n_rows + n_cols + 2 :]
    chunk = tiles.shape[1] // 2
    order = [a for i, (a, _) in enumerate(jobs) if i == 0 or jobs[i - 1][0] != a]

    def loads(turn):
        slot = turn % 2
        return [
            pltpu.make_async_copy(
                row_refs[2 * order[turn] + i], held.at[slot, pl.ds(i * chunk, chunk)], row_sems.at[slot, i]
            )
            for i in range(2)
        ]

    def stores(index):
        a, b = jobs[index]
        slot = index % 2
        half, row_at = row_plan[a]
        kind, col_at = col_plan[b]
        col = pl.multiple_of(base_ref[4 + kind] + col_at, 128)
        out = []
        for i in range(2):
            row = pl.multiple_of(base_ref[2 * half + i] + row_at, 8)
            out.append(
                pltpu.make_async_copy(
                    tiles.at[slot, pl.ds(i * chunk, chunk)],
                    out_ref.at[pl.ds(row, chunk), pl.ds(col, tiles.shape[2])],
                    sems.at[slot, i],
                )
            )
        return out

    for copy in loads(0):
        copy.start()
    for b in range(n_cols):
        block = col_refs[b][...].astype(jnp.float32)
        frame = lax.broadcasted_iota(jnp.int32, block.shape, 1)
        rolled = jnp.where(frame == 0, 0.0, pltpu.roll(block, 1, 1))
        turned[b] = rolled.T.astype(jnp.bfloat16)
    turn = -1
    for index, (a, b) in enumerate(jobs):
        if index == 0 or jobs[index - 1][0] != a:
            turn += 1
            for copy in loads(turn):
                copy.wait()
            if turn + 1 < len(order):
                for copy in loads(turn + 1):
                    copy.start()
        if index >= 2:
            for copy in stores(index - 2):
                copy.wait()
        tiles[index % 2] = scaling * jnp.dot(
            held[turn % 2], turned[b], preferred_element_type=jnp.float32
        )
        for copy in stores(index):
            copy.start()
    for index in range(max(0, len(jobs) - 2), len(jobs)):
        for copy in stores(index):
            copy.wait()


def covariance_part(covariance, base, pairs, scaling):
    rows, cols, jobs = [], [], []
    for row, col in pairs:
        for group, one in ((rows, row), (cols, col)):
            if not any(one is seen for seen in group):
                group.append(one)
        a = next(i for i, seen in enumerate(rows) if seen is row)
        jobs.append((a, next(i for i, seen in enumerate(cols) if seen is col)))
    jobs.sort()
    height, depth = rows[0][0][0].shape
    width = cols[0][0].shape[0]
    vmem, anywhere = pl.BlockSpec(memory_space=pltpu.VMEM), pl.BlockSpec(memory_space=pl.ANY)
    operands = [base, *(part for r in rows for part in r[0]), *(c[0] for c in cols), covariance]
    plan = ([r[1:] for r in rows], [c[1:] for c in cols], jobs)
    tiles = len(jobs) * 2 * height * width
    return pl.pallas_call(
        lambda *refs: tile_kernel(plan, scaling, *refs),
        out_shape=jax.ShapeDtypeStruct(covariance.shape, covariance.dtype),
        in_specs=[pl.BlockSpec(memory_space=pltpu.SMEM)]
        + [anywhere] * (2 * len(rows))
        + [vmem] * len(cols)
        + [anywhere],
        out_specs=anywhere,
        scratch_shapes=[
            pltpu.VMEM((2, 2 * height, depth), jnp.bfloat16),
            pltpu.VMEM((len(cols), depth, width), jnp.bfloat16),
            pltpu.VMEM((2, 2 * height, width), jnp.float32),
            pltpu.SemaphoreType.DMA((2, 2)),
            pltpu.SemaphoreType.DMA((2, 2)),
        ],
        input_output_aliases={len(operands) - 1: 0},
        compiler_params=pltpu.CompilerParams(vmem_limit_bytes=40 * 2**20),
        cost_estimate=pl.CostEstimate(flops=2 * tiles * depth, bytes_accessed=4 * tiles, transcendentals=0),
    )(*operands)


def empty_kernel(out_ref):
    pass


def tie(*values):
    return lax.optimization_barrier(values)


def local(frames, chunks, sizes, interaction, commands, slopes, frame_lag, frame_count):
    n_rows, n_line = sizes
    row = lax.axis_index("rows")
    place = lax.axis_index("line")
    core = lax.axis_index("core")
    all_frames = slopes.shape[1]
    block_rows, block_acts = interaction.shape
    half = block_rows // 2
    quarter = half // 2
    middle = n_line // 2 - 1
    side = (place > middle).astype(jnp.int32)
    inner = (place == middle) | (place == middle + 1)

    def flat(r, z, k):
        return (r * n_line + z) * 2 + k

    def move(value, hops):
        pairs = [(flat(*a), flat(*b)) for a, b in hops]
        return lax.ppermute(value, AXES, pairs)

    everyone = [(r, z, k) for r in range(n_rows) for z in range(n_line) for k in range(2)]

    def swap_core(value):
        return move(value, [((r, z, k), (r, z, 1 - k)) for r, z, k in everyone])

    block_frames = commands.shape[0]
    sources = [r for r in range(n_rows) if r * block_frames < frames]

    def cross(value, mask, wanted):
        return move(value, [((r, z, k), (r ^ mask, z, k)) for r, z, k in everyone if r in wanted])

    n_bits = n_rows.bit_length() - 1
    begun = []
    for bit in range(n_bits):
        begun.append(cross(commands, 1 << bit, sources))
    slab = slopes.shape[0]
    per_quarter = quarter // slab
    for i in range(per_quarter):
        hops = []
        for r in range(n_rows):
            for k in range(2):
                for o in range(2):
                    index = (k * 2 + o) * per_quarter + i
                    hops.append(((r, index // 2, index % 2), (r, middle + o, k)))
        begun.append(move(slopes[:, :frames], hops))
    begun.append(swap_core(interaction))
    begun = lax.optimization_barrier(begun)
    other = begun[-1]
    measured = begun[n_bits:-1]
    blocks = {0: commands}
    blocks.update({1 << bit: begun[bit] for bit in range(n_bits)})
    for mask in range(n_rows):
        ways = [1 << bit for bit in range(n_bits) if mask >> bit & 1]
        if len(ways) < 2:
            continue
        share = block_frames // len(ways)
        shares = [
            cross(blocks[mask ^ way][i * share : (i + 1) * share], way, [r ^ mask ^ way for r in sources])
            for i, way in enumerate(ways)
        ]
        blocks[mask] = jnp.concatenate(shares, 0)
    margin = all_frames // 4
    held = jnp.zeros((margin + n_rows * block_frames, block_acts), commands.dtype)
    for mask, block in blocks.items():
        held = lax.dynamic_update_slice_in_dim(held, block, margin + (row ^ mask) * block_frames, 0)
    delayed = lax.dynamic_slice_in_dim(held, margin - frame_lag[0], frames, 0)
    delayed_other = swap_core(delayed)

    chunk = quarter // chunks

    def response(offset):
        parts = [
            lax.dot_general(
                lax.dynamic_slice_in_dim(matrix, offset + at, chunk, 0),
                command,
                NT,
                preferred_element_type=jnp.float32,
            )
            for matrix, at, command in ((interaction, core * half, delayed), (other, core * half, delayed_other))
        ]
        return parts[0] + parts[1]

    def measured_part(j):
        first, stop = j * chunk, (j + 1) * chunk
        parts = [
            measured[i][max(first - i * slab, 0) : min(stop - i * slab, slab)]
            for i in range(per_quarter)
            if i * slab < stop and first < (i + 1) * slab
        ]
        return parts[0] if len(parts) == 1 else jnp.concatenate(parts, 0)

    last = n_line - 1
    inward = [
        [((r, z, k), (r, z + d, k)) for r in range(n_rows) for k in range(2) for z, d in ((i, 1), (last - i, -1))]
        for i in range(middle)
    ]
    outward = [[(b, a) for a, b in hops] for hops in reversed(inward)]
    across = [
        ((r, middle + o, k), (r, middle + 1 - o, k)) for r in range(n_rows) for k in range(2) for o in range(2)
    ]

    def exchange(value, finished):
        zeros = jnp.zeros((chunk, frames), jnp.bfloat16)
        if middle == 1:
            narrow = zeros if value is None else value.astype(jnp.bfloat16)
            moved = move(jnp.where(inner, zeros if finished is None else finished, narrow), inward[0] + outward[0])
            return moved, moved
        added = value
        if value is not None:
            for hops in inward:
                arrived = move(added.astype(jnp.bfloat16), hops)
                added = value + arrived.astype(jnp.float32)
        if finished is not None:
            for step, hops in enumerate(outward):
                reached = jnp.where(side == 1, place - middle - 1, middle - place)
                finished = jnp.where(reached == step + 1, move(finished, hops), finished)
        return (None if value is None else arrived), finished

    per_row = 2 * n_line // n_rows
    source = (2 * place + core) // per_row

    def spread(value, bit):
        step = 1 << bit
        hops = []
        for z in range(n_line):
            for k in range(2):
                s = (2 * z + k) // per_row
                hops += [((s ^ m, z, k), (s ^ m ^ step, z, k)) for m in range(step)]
        return jnp.where((row ^ source) // step == 1, move(value, hops), value)

    frame_index = lax.broadcasted_iota(jnp.int32, (chunk, frames), 1)
    valid = frame_index < frame_count[0]
    scaling = 1.0 / math.sqrt(all_frames)
    n_columns = n_rows * block_rows // (2 * n_line)
    pieces = half // n_columns
    covariance = pl.pallas_call(
        empty_kernel,
        out_shape=jax.ShapeDtypeStruct((block_rows, n_columns), jnp.float32),
        out_specs=pl.BlockSpec(memory_space=pl.ANY),
    )()
    near_at, far_at = side * quarter, (1 - side) * quarter
    own_at, other_at = core * half, (1 - core) * half
    column_at = (near_at, far_at) if pieces == 1 else (0, 0)
    base = jnp.stack(
        [own_at + near_at, own_at + far_at, other_at + near_at, other_at + far_at, *column_at]
    ).astype(jnp.int32)

    live = {
        "far": response(far_at),
        "covariance": covariance,
    }
    row_info, col_info, waiting = {}, {}, []
    n_steps = 2 * chunks + 2 + n_bits + (0 if pieces == 1 else 1)
    for h in range(n_steps + 1):
        tied = [key for key in live if frames == all_frames or key[0] not in FREE]
        live.update(zip(tied, lax.optimization_barrier([live[key] for key in tied])))
        j, odd = h // 2, h % 2
        new = dict(live)
        into = live.pop("near" if odd else "far", None)
        new.pop("near" if odd else "far", None)
        finished = None
        if odd and j < chunks:
            total = live["far_value"] + live["arrived"].astype(jnp.float32)
            new.pop("far_value")
            new["crossed"] = move(total.astype(jnp.bfloat16), across)
        if odd and 1 <= j <= chunks:
            finished = new.pop("other_done")
        if not odd and 1 <= j <= chunks:
            part = measured_part(j - 1).astype(jnp.float32)
            total = live["near_value"] + live["arrived"].astype(jnp.float32)
            total = total + live["crossed"].astype(jnp.float32) + part
            for name in ("near_value", "crossed"):
                new.pop(name)
            finished = jnp.where(valid, total, 0.0).astype(jnp.bfloat16)
            new["other_done"] = move(finished, across)
        new.pop("arrived", None)
        if into is not None or finished is not None:
            arrived, done = exchange(into, finished)
            if into is not None:
                new["arrived"] = arrived
                new["near_value" if odd else "far_value"] = into
            if finished is not None:
                mine = finished if middle == 1 else None
                done = done if mine is None else jnp.where(inner, mine, done)
                new[("far_rows" if odd else "near_rows", j - 1)] = done
        for name, key, i in (("near_rows", 0, (h - 3) // 2), ("far_rows", 1, (h - 4) // 2)):
            if h >= 3 and (h % 2 == 1) == (key == 0) and 0 <= i < chunks:
                new["row", 0, i, key] = live[name, i]
                new["row", 1, i, key] = swap_core(live[name, i])
        if pieces == 1:
            begun = [(("near_rows", (h - 3) // 2), h >= 3 and odd), (("far_rows", (h - 4) // 2), h >= 4 and not odd)]
            for (name, i), now in begun:
                if now and i < chunks:
                    waiting.append([live[name, i], 0, int(name == "far_rows"), i])
        else:
            i = (h - 5) // 2
            if h >= 5 and odd and i < chunks:
                wanted = (2 * place + core) % per_row
                parts = [
                    jnp.where(wanted // pieces == core, live["row", 0, i, part], live["row", 1, i, part])
                    for part in range(2)
                ]
                waiting.append([jnp.where(wanted % pieces == side, *parts), 0, 0, i])
        for name in [key for key in live if key[0] == "moving"]:
            waiting.append([live[name], *name[1:]])
            new.pop(name)
        for value, bit, kind, i in waiting:
            value = spread(value, bit)
            new[("col", kind, i) if bit + 1 == n_bits else ("moving", bit + 1, kind, i)] = value
        waiting = []
        if j < chunks and not odd:
            new["near"] = response(near_at + j * chunk)
        if odd and j + 1 < chunks:
            new["far"] = response(far_at + (j + 1) * chunk)
        row_keys = [key[:3] for key in live if key[0] == "row" and key[3] == 1]
        col_keys = [key for key in live if key[0] == "col"]
        row_of = {key: ((live[*key, 0], live[*key, 1]), key[1], key[2] * chunk) for key in row_keys}
        col_of = {key: (live[key], key[1], key[2] * chunk) for key in col_keys}
        todo = [
            (row_of[a], col_of[b]) for b in col_keys for a in row_keys if (a, b) not in row_info
        ]
        row_info.update({(a, b): True for b in col_keys for a in row_keys})
        if todo:
            new["covariance"] = covariance_part(live["covariance"], base, todo, scaling)
        live = new
    return live["covariance"]


def solution(mesh, force=None, chunks=2):
    n_rows, n_cols = mesh.devices.shape
    line = Mesh(mesh.devices.reshape(n_rows, n_cols // 2, 2), AXES)
    sizes = (n_rows, n_cols // 2)

    def body(interaction, commands, slopes, frame_lag, frame_count):
        args = (interaction, commands, slopes, frame_lag, frame_count)
        unit = slopes.shape[1] // 4
        if force is not None:
            return local(force, chunks, sizes, *args)
        extents = [unit * i for i in range(2, 5)]
        which = jnp.clip((frame_count[0] + unit - 1) // unit - 2, 0, len(extents) - 1)
        return lax.switch(which, [partial(local, frames, chunks, sizes) for frames in extents], *args)

    both = ("line", "core")
    return jax.shard_map(
        body,
        mesh=line,
        in_specs=(P("rows", both), P("rows", both), P(AXES, None), P(), P()),
        out_specs=P("rows", both),
        check_vma=False,
    )
```

```python
import math
from functools import partial

import jax
import jax.numpy as jnp
import numpy as np
from jax import lax
from jax.experimental import pallas as pl
from jax.experimental.pallas import tpu as pltpu
from jax.sharding import Mesh, PartitionSpec as P

AXES = ("rows", "line", "core")
FREE = ("row", "col", "moving", "near_rows", "far_rows")
NT = (((1,), (1,)), ((), ()))


def tile_kernel(plan, scaling, base_ref, *refs):
    row_plan, col_plan, jobs = plan
    n_rows, n_cols = len(row_plan), len(col_plan)
    row_refs = refs[: 2 * n_rows]
    col_refs = refs[2 * n_rows : 2 * n_rows + n_cols]
    out_ref = refs[2 * n_rows + n_cols + 1]
    held, turned, tiles, row_sems, sems = refs[2 * n_rows + n_cols + 2 :]
    chunk = tiles.shape[1] // 2
    order = [a for i, (a, _) in enumerate(jobs) if i == 0 or jobs[i - 1][0] != a]

    def loads(turn):
        slot = turn % 2
        return [
            pltpu.make_async_copy(
                row_refs[2 * order[turn] + i], held.at[slot, pl.ds(i * chunk, chunk)], row_sems.at[slot, i]
            )
            for i in range(2)
        ]

    def stores(index):
        a, b = jobs[index]
        slot = index % 2
        half, row_at = row_plan[a]
        kind, col_at = col_plan[b]
        col = pl.multiple_of(base_ref[4 + kind] + col_at, 128)
        out = []
        for i in range(2):
            row = pl.multiple_of(base_ref[2 * half + i] + row_at, 8)
            out.append(
                pltpu.make_async_copy(
                    tiles.at[slot, pl.ds(i * chunk, chunk)],
                    out_ref.at[pl.ds(row, chunk), pl.ds(col, tiles.shape[2])],
                    sems.at[slot, i],
                )
            )
        return out

    for copy in loads(0):
        copy.start()
    for b in range(n_cols):
        block = col_refs[b][...].astype(jnp.float32)
        frame = lax.broadcasted_iota(jnp.int32, block.shape, 1)
        rolled = jnp.where(frame == 0, 0.0, pltpu.roll(block, 1, 1))
        turned[b] = rolled.T.astype(jnp.bfloat16)
    turn = -1
    for index, (a, b) in enumerate(jobs):
        if index == 0 or jobs[index - 1][0] != a:
            turn += 1
            for copy in loads(turn):
                copy.wait()
            if turn + 1 < len(order):
                for copy in loads(turn + 1):
                    copy.start()
        if index >= 2:
            for copy in stores(index - 2):
                copy.wait()
        tiles[index % 2] = scaling * jnp.dot(
            held[turn % 2], turned[b], preferred_element_type=jnp.float32
        )
        for copy in stores(index):
            copy.start()
    for index in range(max(0, len(jobs) - 2), len(jobs)):
        for copy in stores(index):
            copy.wait()


def covariance_part(covariance, base, pairs, scaling):
    rows, cols, jobs = [], [], []
    for row, col in pairs:
        for group, one in ((rows, row), (cols, col)):
            if not any(one is seen for seen in group):
                group.append(one)
        a = next(i for i, seen in enumerate(rows) if seen is row)
        jobs.append((a, next(i for i, seen in enumerate(cols) if seen is col)))
    jobs.sort()
    height, depth = rows[0][0][0].shape
    width = cols[0][0].shape[0]
    vmem, anywhere = pl.BlockSpec(memory_space=pltpu.VMEM), pl.BlockSpec(memory_space=pl.ANY)
    operands = [base, *(part for r in rows for part in r[0]), *(c[0] for c in cols), covariance]
    plan = ([r[1:] for r in rows], [c[1:] for c in cols], jobs)
    tiles = len(jobs) * 2 * height * width
    return pl.pallas_call(
        lambda *refs: tile_kernel(plan, scaling, *refs),
        out_shape=jax.ShapeDtypeStruct(covariance.shape, covariance.dtype),
        in_specs=[pl.BlockSpec(memory_space=pltpu.SMEM)]
        + [anywhere] * (2 * len(rows))
        + [vmem] * len(cols)
        + [anywhere],
        out_specs=anywhere,
        scratch_shapes=[
            pltpu.VMEM((2, 2 * height, depth), jnp.bfloat16),
            pltpu.VMEM((len(cols), depth, width), jnp.bfloat16),
            pltpu.VMEM((2, 2 * height, width), jnp.float32),
            pltpu.SemaphoreType.DMA((2, 2)),
            pltpu.SemaphoreType.DMA((2, 2)),
        ],
        input_output_aliases={len(operands) - 1: 0},
        compiler_params=pltpu.CompilerParams(vmem_limit_bytes=40 * 2**20),
        cost_estimate=pl.CostEstimate(flops=2 * tiles * depth, bytes_accessed=4 * tiles, transcendentals=0),
    )(*operands)


def empty_kernel(out_ref):
    pass


def tie(*values):
    return lax.optimization_barrier(values)


def local(frames, chunks, sizes, interaction, commands, slopes, frame_lag, frame_count):
    n_rows, n_line = sizes
    row = lax.axis_index("rows")
    place = lax.axis_index("line")
    core = lax.axis_index("core")
    all_frames = slopes.shape[1]
    block_rows, block_acts = interaction.shape
    half = block_rows // 2
    quarter = half // 2
    middle = n_line // 2 - 1
    side = (place > middle).astype(jnp.int32)
    inner = (place == middle) | (place == middle + 1)

    def flat(r, z, k):
        return (r * n_line + z) * 2 + k

    def move(value, hops):
        pairs = [(flat(*a), flat(*b)) for a, b in hops]
        return lax.ppermute(value, AXES, pairs)

    everyone = [(r, z, k) for r in range(n_rows) for z in range(n_line) for k in range(2)]

    def swap_core(value):
        return move(value, [((r, z, k), (r, z, 1 - k)) for r, z, k in everyone])

    block_frames = commands.shape[0]
    sources = [r for r in range(n_rows) if r * block_frames < frames]

    def cross(value, mask, wanted):
        return move(value, [((r, z, k), (r ^ mask, z, k)) for r, z, k in everyone if r in wanted])

    n_bits = n_rows.bit_length() - 1
    begun = []
    for bit in range(n_bits):
        begun.append(cross(commands, 1 << bit, sources))
    slab = slopes.shape[0]
    per_quarter = quarter // slab
    for i in range(per_quarter):
        hops = []
        for r in range(n_rows):
            for k in range(2):
                for o in range(2):
                    index = (k * 2 + o) * per_quarter + i
                    hops.append(((r, index // 2, index % 2), (r, middle + o, k)))
        begun.append(move(slopes[:, :frames], hops))
    begun.append(swap_core(interaction))
    begun = lax.optimization_barrier(begun)
    other = begun[-1]
    measured = begun[n_bits:-1]
    blocks = {0: commands}
    blocks.update({1 << bit: begun[bit] for bit in range(n_bits)})
    for mask in range(n_rows):
        ways = [1 << bit for bit in range(n_bits) if mask >> bit & 1]
        if len(ways) < 2:
            continue
        share = block_frames // len(ways)
        shares = [
            cross(blocks[mask ^ way][i * share : (i + 1) * share], way, [r ^ mask ^ way for r in sources])
            for i, way in enumerate(ways)
        ]
        blocks[mask] = jnp.concatenate(shares, 0)
    margin = all_frames // 4
    held = jnp.zeros((margin + n_rows * block_frames, block_acts), commands.dtype)
    for mask, block in blocks.items():
        held = lax.dynamic_update_slice_in_dim(held, block, margin + (row ^ mask) * block_frames, 0)
    delayed = lax.dynamic_slice_in_dim(held, margin - frame_lag[0], frames, 0)
    delayed_other = swap_core(delayed)

    chunk = quarter // chunks

    def response(offset):
        parts = [
            lax.dot_general(
                lax.dynamic_slice_in_dim(matrix, offset + at, chunk, 0),
                command,
                NT,
                preferred_element_type=jnp.float32,
            )
            for matrix, at, command in ((interaction, core * half, delayed), (other, core * half, delayed_other))
        ]
        return parts[1] + parts[0]

    def measured_part(j):
        first, stop = j * chunk, (j + 1) * chunk
        parts = [
            measured[i][max(first - i * slab, 0) : min(stop - i * slab, slab)]
            for i in range(per_quarter)
            if i * slab < stop and first < (i + 1) * slab
        ]
        return parts[0] if len(parts) == 1 else jnp.concatenate(parts, 0)

    last = n_line - 1
    inward = [
        [((r, z, k), (r, z + d, k)) for r in range(n_rows) for k in range(2) for z, d in ((i, 1), (last - i, -1))]
        for i in range(middle)
    ]
    outward = [[(b, a) for a, b in hops] for hops in reversed(inward)]
    across = [
        ((r, middle + o, k), (r, middle + 1 - o, k)) for r in range(n_rows) for k in range(2) for o in range(2)
    ]

    def exchange(value, finished):
        zeros = jnp.zeros((chunk, frames), jnp.bfloat16)
        if middle == 1:
            narrow = zeros if value is None else value.astype(jnp.bfloat16)
            moved = move(jnp.where(inner, zeros if finished is None else finished, narrow), inward[0] + outward[0])
            return moved, moved
        added = value
        if value is not None:
            for hops in inward:
                arrived = move(added.astype(jnp.bfloat16), hops)
                added = value + arrived.astype(jnp.float32)
        if finished is not None:
            for step, hops in enumerate(outward):
                reached = jnp.where(side == 1, place - middle - 1, middle - place)
                finished = jnp.where(reached == step + 1, move(finished, hops), finished)
        return (None if value is None else arrived), finished

    per_row = 2 * n_line // n_rows
    source = (2 * place + core) // per_row

    def spread(value, bit):
        step = 1 << bit
        hops = []
        for z in range(n_line):
            for k in range(2):
                s = (2 * z + k) // per_row
                hops += [((s ^ m, z, k), (s ^ m ^ step, z, k)) for m in range(step)]
        return jnp.where((row ^ source) // step == 1, move(value, hops), value)

    frame_index = lax.broadcasted_iota(jnp.int32, (chunk, frames), 1)
    valid = frame_index < frame_count[0]
    scaling = 1.0 / math.sqrt(all_frames)
    n_columns = n_rows * block_rows // (2 * n_line)
    pieces = half // n_columns
    covariance = pl.pallas_call(
        empty_kernel,
        out_shape=jax.ShapeDtypeStruct((block_rows, n_columns), jnp.float32),
        out_specs=pl.BlockSpec(memory_space=pl.ANY),
    )()
    near_at, far_at = side * quarter, (1 - side) * quarter
    own_at, other_at = core * half, (1 - core) * half
    column_at = (near_at, far_at) if pieces == 1 else (0, 0)
    base = jnp.stack(
        [own_at + near_at, own_at + far_at, other_at + near_at, other_at + far_at, *column_at]
    ).astype(jnp.int32)

    live = {
        "far": response(far_at),
        "covariance": covariance,
    }
    row_info, col_info, waiting = {}, {}, []
    n_steps = 2 * chunks + 2 + n_bits + (0 if pieces == 1 else 1)
    for h in range(n_steps + 1):
        tied = [key for key in live if frames == all_frames or key[0] not in FREE]
        live.update(zip(tied, lax.optimization_barrier([live[key] for key in tied])))
        j, odd = h // 2, h % 2
        new = dict(live)
        into = live.pop("near" if odd else "far", None)
        new.pop("near" if odd else "far", None)
        finished = None
        if odd and j < chunks:
            total = live["far_value"] + live["arrived"].astype(jnp.float32)
            new.pop("far_value")
            new["crossed"] = move(total.astype(jnp.bfloat16), across)
        if odd and 1 <= j <= chunks:
            finished = new.pop("other_done")
        if not odd and 1 <= j <= chunks:
            part = measured_part(j - 1).astype(jnp.float32)
            total = live["near_value"] + live["arrived"].astype(jnp.float32)
            total = total + live["crossed"].astype(jnp.float32) + part
            for name in ("near_value", "crossed"):
                new.pop(name)
            finished = jnp.where(valid, total, 0.0).astype(jnp.bfloat16)
            new["other_done"] = move(finished, across)
        new.pop("arrived", None)
        if into is not None or finished is not None:
            arrived, done = exchange(into, finished)
            if into is not None:
                new["arrived"] = arrived
                new["near_value" if odd else "far_value"] = into
            if finished is not None:
                mine = finished if middle == 1 else None
                done = done if mine is None else jnp.where(inner, mine, done)
                new[("far_rows" if odd else "near_rows", j - 1)] = done
        for name, key, i in (("near_rows", 0, (h - 3) // 2), ("far_rows", 1, (h - 4) // 2)):
            if h >= 3 and (h % 2 == 1) == (key == 0) and 0 <= i < chunks:
                new["row", 0, i, key] = live[name, i]
                new["row", 1, i, key] = swap_core(live[name, i])
        if pieces == 1:
            begun = [(("near_rows", (h - 3) // 2), h >= 3 and odd), (("far_rows", (h - 4) // 2), h >= 4 and not odd)]
            for (name, i), now in begun:
                if now and i < chunks:
                    waiting.append([live[name, i], 0, int(name == "far_rows"), i])
        else:
            i = (h - 5) // 2
            if h >= 5 and odd and i < chunks:
                wanted = (2 * place + core) % per_row
                parts = [
                    jnp.where(wanted // pieces == core, live["row", 0, i, part], live["row", 1, i, part])
                    for part in range(2)
                ]
                waiting.append([jnp.where(wanted % pieces == side, *parts), 0, 0, i])
        for name in [key for key in live if key[0] == "moving"]:
            waiting.append([live[name], *name[1:]])
            new.pop(name)
        for value, bit, kind, i in waiting:
            value = spread(value, bit)
            new[("col", kind, i) if bit + 1 == n_bits else ("moving", bit + 1, kind, i)] = value
        waiting = []
        if j < chunks and not odd:
            new["near"] = response(near_at + j * chunk)
        if odd and j + 1 < chunks:
            new["far"] = response(far_at + (j + 1) * chunk)
        row_keys = [key[:3] for key in live if key[0] == "row" and key[3] == 1]
        col_keys = [key for key in live if key[0] == "col"]
        row_of = {key: ((live[*key, 0], live[*key, 1]), key[1], key[2] * chunk) for key in row_keys}
        col_of = {key: (live[key], key[1], key[2] * chunk) for key in col_keys}
        todo = [
            (row_of[a], col_of[b]) for b in col_keys for a in row_keys if (a, b) not in row_info
        ]
        row_info.update({(a, b): True for b in col_keys for a in row_keys})
        if todo:
            new["covariance"] = covariance_part(live["covariance"], base, todo, scaling)
        live = new
    return live["covariance"]


def solution(mesh, force=None, chunks=2):
    n_rows, n_cols = mesh.devices.shape
    line = Mesh(mesh.devices.reshape(n_rows, n_cols // 2, 2), AXES)
    sizes = (n_rows, n_cols // 2)

    def body(interaction, commands, slopes, frame_lag, frame_count):
        args = (interaction, commands, slopes, frame_lag, frame_count)
        unit = slopes.shape[1] // 4
        if force is not None:
            return local(force, chunks, sizes, *args)
        extents = [unit * i for i in range(2, 5)]
        which = jnp.clip((frame_count[0] + unit - 1) // unit - 2, 0, len(extents) - 1)
        return lax.switch(which, [partial(local, frames, chunks, sizes) for frames in extents], *args)

    both = ("line", "core")
    return jax.shard_map(
        body,
        mesh=line,
        in_specs=(P("rows", both), P("rows", both), P(AXES, None), P(), P()),
        out_specs=P("rows", both),
        check_vma=False,
    )
```
